256 devices in a mesh: row: 16 (over y, x), col: 8 (over z), depth: 2 (over core).
Axes of the slice: x: 4, y: 4, z: 8, core: 2. Of those that a mesh axis runs over, the one named last changes fastest.
Arguments:
- ham_blocks: bfloat16 [512, 8, 128, 128], P(('row', 'depth'), 'col'), may hold values from -0.25 to 0.25
- deriv_blocks: bfloat16 [512, 8, 128, 128], P(('row', 'depth'), 'col'), may hold values from -0.25 to 0.25
- ham_cols: int32 [512, 8], P(('row', 'depth')), may hold values from 0 to 511, as said below
- cheb_prev: bfloat16 [32, 64, 128, 128], P('col', 'row'), may hold values from -6 to 6
- cheb_cur: bfloat16 [32, 64, 128, 128], P('col', 'row'), may hold values from -6 to 6
- tang_prev: bfloat16 [32, 64, 128, 128], P('col', 'row'), may hold values from -6 to 6
- tang_cur: bfloat16 [32, 64, 128, 128], P('col', 'row'), may hold values from -6 to 6
- cheb_rows: int32 [32, 64], P('col'), may hold values from 0 to 511, as said below
- keep_mask: int32 [32, 64], P('col', 'row'), may hold values 0 or 1
Outputs:
- cheb_last: bfloat16 [32, 64, 128, 128], P('col', 'row')
- tang_last: bfloat16 [32, 64, 128, 128], P('col', 'row')
The draws below stay inside these ranges and needn't reach their ends.
Inputs may be any that keep to these rules, and one draw needn't show every extreme that they name: `ham_cols`: each block row lists 8 different block columns, 1 of them in each of the 8 ranges of 64 columns, the ranges in order along the slots. `cheb_rows`: each window column lists 64 different block rows, 2 of them in each of the 32 ranges of 16 rows, the ranges in order along the slots.
All inputs are finite; a program needn't handle non-finite values. No bound on the sum of `keep_mask` on one device may be relied on, other than what follows from the above.
Results may differ from the reference program's by a relative error of at most 0.0042.
Values may be sent and summed in bfloat16 or wider, within the bound.
No kernel may reach another device: no remote copies, remote signals or barrier semaphores. Data moves between devices by JAX's collectives and lax.ppermute only.
A program may use at most 128 MiB of HBM per device.

```python
import jax
import jax.numpy as jnp
from jax import lax

NB = 512
BS = 128
SH = 8
ST = 64
NBC = 32
GRID_COLS = 8
LAYER_GROUPS = 32
COLW = 64
HGRP = 1
RGRP = 16
SGRP = 2


def draw_ham_cols(key, part):
    key = jax.random.fold_in(key, 11)
    scores = jax.random.randint(key, (NB, GRID_COLS, COLW), 0, 1 << 20)
    scores = scores * COLW + jnp.arange(COLW, dtype=jnp.int32)[None, None, :]
    scores = scores.at[0, 0, 0].set(-1)
    scores = scores.at[0, GRID_COLS - 1, COLW - 1].set(-1)
    order = jnp.argsort(scores, axis=-1)[:, :, :HGRP].astype(jnp.int32)
    starts = (jnp.arange(GRID_COLS, dtype=jnp.int32) * COLW)[None, :, None]
    return (order + starts).reshape(NB, SH).astype(jnp.int32)


def draw_cheb_rows(key, part):
    key = jax.random.fold_in(key, 23)
    scores = jax.random.randint(key, (NBC, LAYER_GROUPS, RGRP), 0, 1 << 20)
    scores = scores * RGRP + jnp.arange(RGRP, dtype=jnp.int32)[None, None, :]
    scores = scores.at[0, 0, 0].set(-1)
    scores = scores.at[0, LAYER_GROUPS - 1, RGRP - 1].set(-1)
    order = jnp.argsort(scores, axis=-1)[:, :, :SGRP].astype(jnp.int32)
    starts = (jnp.arange(LAYER_GROUPS, dtype=jnp.int32) * RGRP)[None, :, None]
    return (order + starts).reshape(NBC, ST).astype(jnp.int32)


def place_ends(values, stream_key, least, top_value):
    index_at = [jax.random.randint(jax.random.fold_in(stream_key, axis), (), 0, length) for axis, length in enumerate(values.shape)]
    widest = values.shape.index(max(values.shape))
    beside = index_at[:widest] + [(index_at[widest] + 1) % values.shape[widest]] + index_at[widest + 1:]
    return values.at[tuple(index_at)].set(least).at[tuple(beside)].set(top_value)


def steps_of(stream_key, shape, shards, smallest, high):
    level = 1.0
    for dim, blocks in shards:
        steps = jax.random.uniform(jax.random.fold_in(jax.random.fold_in(stream_key, 6), dim), (blocks,), jnp.float32, smallest / len(shards), high / len(shards))
        level = level * jnp.repeat(jnp.exp(steps), shape[dim] // blocks).reshape((-1,) + (1,) * (len(shape) - 1 - dim))
    return level


def scatter_about(rng, dims, spread, most, pieces=(), kind=jnp.bfloat16):
    result = jax.random.normal(rng, dims, jnp.float32) * spread
    if len(pieces) > 0:
        result = steps_of(rng, dims, pieces, -0.22, 0.18) * result
    return jnp.clip(result, min=-most, max=most).astype(kind)


def setup_inputs(seed: int = 0) -> dict:
    seeds = jax.random.split(jax.random.key(seed), 10)
    ham_blocks = scatter_about(seeds[0], (NB, SH, BS, BS), (4 * BS) ** -0.5, 0.25, ((0, 32), (1, 8)))
    deriv_blocks = scatter_about(seeds[1], (NB, SH, BS, BS), (4 * BS) ** -0.5, 0.25, ((0, 32), (1, 8)))
    ham_cols = draw_ham_cols(jax.random.fold_in(seeds[9], 71), 0)
    cheb_prev = scatter_about(seeds[3], (NBC, ST, BS, BS), 1.0, 6.0, ((0, 8), (1, 16)))
    cheb_cur = scatter_about(seeds[4], (NBC, ST, BS, BS), 1.0, 6.0, ((0, 8), (1, 16)))
    tang_prev = scatter_about(seeds[5], (NBC, ST, BS, BS), 1.0, 6.0, ((0, 8), (1, 16)))
    tang_cur = scatter_about(seeds[6], (NBC, ST, BS, BS), 1.0, 6.0, ((0, 8), (1, 16)))
    cheb_rows = draw_cheb_rows(jax.random.fold_in(seeds[9], 71), 0)
    keep_mask = place_ends((jax.random.randint(seeds[8], (NBC, ST), 0, 8) < 7).astype(jnp.int32), jax.random.fold_in(seeds[8], 1), 0, 1)
    return dict(ham_blocks=ham_blocks, deriv_blocks=deriv_blocks, ham_cols=ham_cols, cheb_prev=cheb_prev, cheb_cur=cheb_cur, tang_prev=tang_prev, tang_cur=tang_cur, cheb_rows=cheb_rows, keep_mask=keep_mask)


def column_products(ham_blocks, deriv_blocks, ham_cols, cheb_col, tang_col, rows):
    needed = jnp.take(ham_cols, rows, axis=0)
    equal = needed[:, :, None] == rows[None, None, :]
    found = jnp.any(equal, axis=-1)
    position = jnp.argmax(equal, axis=-1).astype(jnp.int32)
    mask = found[:, :, None, None]
    picked_cheb = jnp.where(mask, jnp.take(cheb_col, position, axis=0), 0).astype(jnp.float32)
    picked_tang = jnp.where(mask, jnp.take(tang_col, position, axis=0), 0).astype(jnp.float32)
    picked_ham = jnp.take(ham_blocks, rows, axis=0).astype(jnp.float32)
    picked_deriv = jnp.take(deriv_blocks, rows, axis=0).astype(jnp.float32)
    high = lax.Precision.HIGHEST
    prod_cheb = jnp.einsum('sqab,sqbc->sac', picked_ham, picked_cheb, precision=high)
    prod_tang = jnp.einsum('sqab,sqbc->sac', picked_deriv, picked_cheb, precision=high)
    prod_tang = prod_tang + jnp.einsum('sqab,sqbc->sac', picked_ham, picked_tang, precision=high)
    return prod_cheb, prod_tang


def advance(ham_blocks, deriv_blocks, ham_cols, cheb_rows, keep_mask, cheb_now, tang_now, cheb_old, tang_old):
    def one_column(items):
        return column_products(ham_blocks, deriv_blocks, ham_cols, items[0], items[1], items[2])

    prod_cheb, prod_tang = lax.map(one_column, (cheb_now, tang_now, cheb_rows))
    keep = keep_mask.astype(jnp.float32)[:, :, None, None]
    cheb_new = (keep * (2.0 * prod_cheb - cheb_old.astype(jnp.float32))).astype(jnp.bfloat16)
    tang_new = (keep * (2.0 * prod_tang - tang_old.astype(jnp.float32))).astype(jnp.bfloat16)
    return cheb_new, tang_new


def reference(ham_blocks, deriv_blocks, ham_cols, cheb_prev, cheb_cur, tang_prev, tang_cur, cheb_rows, keep_mask):
    cheb_mid, tang_mid = advance(ham_blocks, deriv_blocks, ham_cols, cheb_rows, keep_mask, cheb_cur, tang_cur, cheb_prev, tang_prev)
    cheb_last, tang_last = advance(ham_blocks, deriv_blocks, ham_cols, cheb_rows, keep_mask, cheb_mid, tang_mid, cheb_cur, tang_cur)
    return cheb_last, tang_last
```

```python
import functools

import jax
import jax.numpy as jnp
from jax import lax
from jax.experimental import pallas as pl
from jax.experimental.pallas import tpu as pltpu
from jax.sharding import PartitionSpec as P

ROWS, COLS, CORES = 16, 8, 2


def ring(shift):
    return [(i, (i + shift) % COLS) for i in range(COLS)]


def z_ring(blocks):
    half = blocks.shape[0] // 2
    up, down = [blocks], [blocks]
    for _ in range(3):
        up.append(lax.ppermute(up[-1], "col", ring(1)))
        down.append(lax.ppermute(down[-1], "col", ring(-1)))
    far_low = lax.ppermute(up[-1][:half], "col", ring(1))
    far_high = lax.ppermute(down[-1][half:], "col", ring(-1))
    pieces = [None] * COLS
    pieces[0] = [blocks]
    for step in range(1, 4):
        pieces[COLS - step] = [up[step]]
        pieces[step] = [down[step]]
    pieces[4] = [far_low, far_high]
    return pieces


def swap(array):
    return lax.ppermute(array, "depth", [(0, 1), (1, 0)])


def combine_kernel(pos, rowin, tpos, keep, *refs):
    ham = refs[:36]
    panel, cheb_old, tang_old, cheb_new, tang_new, buf, acc, sems = refs[36:]

    def parts(kind, owner, z):
        base = (kind * 2 + owner) * 9
        if z == 4:
            return ham[base + 7], ham[base + 8]
        return (ham[base + (z if z < 4 else z - 1)],)

    def ham_copy(ref, row, slot, kind):
        return pltpu.make_async_copy(ref.at[row], buf.at[slot, kind], sems.at[slot, kind])

    def panel_copy(place, out, slot, kind):
        column = lax.shift_right_logical(out, 1) & 1
        source = panel.at[lax.shift_right_logical(place, 2), kind, column, place & 3]
        return pltpu.make_async_copy(source, buf.at[slot, 2 + kind], sems.at[slot, 2 + kind])

    for owner in range(2):
        for z in range(COLS):

            def issue(i, carry, owner=owner, z=z):
                out = owner * 4 + i
                slot = out * COLS + z
                place = pos[slot]

                @pl.when(place >= 0)
                def _():
                    row = rowin[out]
                    for kind in range(2):
                        panel_copy(place, out, slot, kind).start()
                        refs_z = parts(kind, owner, z)
                        if len(refs_z) == 1:
                            ham_copy(refs_z[0], row, slot, kind).start()
                        else:

                            @pl.when(row < 8)
                            def _(kind=kind, refs_z=refs_z):
                                ham_copy(refs_z[0], row, slot, kind).start()

                            @pl.when(row >= 8)
                            def _(kind=kind, refs_z=refs_z):
                                ham_copy(refs_z[1], row - 8, slot, kind).start()

                return carry

            lax.fori_loop(0, 4, issue, 0)

    acc[...] = jnp.zeros_like(acc)

    def work(slot, carry):
        @pl.when(pos[slot] >= 0)
        def _():
            out = lax.shift_right_logical(slot, 3)
            for kind in range(2):
                ham_copy(ham[0], 0, slot, kind).wait()
                panel_copy(0, 0, slot, kind).wait()
            h, d, x, t = (buf[slot, i] for i in range(4))
            dot = functools.partial(jnp.dot, preferred_element_type=jnp.float32)
            acc[out, 0] += dot(h, x)
            acc[out, 1] += dot(d, x) + dot(h, t)

        return carry

    lax.fori_loop(0, 64, work, 0)

    def finish(out, carry):
        column = lax.shift_right_logical(out, 1) & 1
        t = tpos[out]
        scale = keep[out].astype(jnp.float32)
        old = cheb_old[column, t].astype(jnp.float32)
        cheb_new[column, t] = (scale * (2.0 * acc[out, 0] - old)).astype(jnp.bfloat16)
        old = tang_old[column, t].astype(jnp.float32)
        tang_new[column, t] = (scale * (2.0 * acc[out, 1] - old)).astype(jnp.bfloat16)
        return carry

    lax.fori_loop(0, 8, finish, 0)


def combine(tables, ham_pieces, panel, cheb_old, tang_old):
    any_space = pl.BlockSpec(memory_space=pl.ANY)
    vmem = pl.BlockSpec(memory_space=pltpu.VMEM)
    smem = pl.BlockSpec(memory_space=pltpu.SMEM)
    shape = jax.ShapeDtypeStruct(cheb_old.shape, jnp.bfloat16)
    return pl.pallas_call(
        combine_kernel,
        out_shape=(shape, shape),
        in_specs=[smem] * 4 + [any_space] * 37 + [vmem] * 2,
        out_specs=(vmem, vmem),
        scratch_shapes=[
            pltpu.VMEM((64, 4, 128, 128), jnp.bfloat16),
            pltpu.VMEM((8, 2, 128, 128), jnp.float32),
            pltpu.SemaphoreType.DMA((64, 4)),
        ],
        compiler_params=pltpu.CompilerParams(vmem_limit_bytes=24 * 1024 * 1024),
        cost_estimate=pl.CostEstimate(flops=100_000_000, bytes_accessed=4_000_000, transcendentals=0),
    )(*tables, *ham_pieces, panel, cheb_old, tang_old)


def needs(my_rows, ham_cols, other_cols, row_group, layer, col):
    rows = lax.dynamic_slice_in_dim(my_rows, row_group * 4, 4, 1)
    by_group = rows.reshape(2, 2, 2).transpose(1, 0, 2)
    by_owner = jnp.where(layer == 0, by_group, by_group[::-1])
    group = jnp.stack([layer, 1 - layer])
    row_in = by_owner - row_group * 32 - 16 * group[:, None, None]
    cols = jnp.stack([ham_cols, other_cols])
    onehot = row_in[..., None] == jnp.arange(16, dtype=jnp.int32)
    needed = jnp.sum(jnp.where(onehot[..., None], cols[:, None, None], 0), axis=3)
    order = (col + jnp.arange(8, dtype=jnp.int32)) % 8
    turn = order[:, None] == jnp.arange(8, dtype=jnp.int32)
    needed = jnp.sum(jnp.where(turn, needed[..., None, :], 0), axis=-1)
    equal = needed[..., None] == my_rows[None, :, None, None, :]
    place = jnp.max(jnp.where(equal, jnp.arange(64, dtype=jnp.int32), -1), axis=-1)
    return place, row_in, group


def on_device(
    ham_blocks,
    deriv_blocks,
    ham_cols,
    cheb_prev,
    cheb_cur,
    tang_prev,
    tang_cur,
    cheb_rows,
    keep_mask,
):
    layer = lax.axis_index("depth")
    row_group = lax.axis_index("row")
    col = lax.axis_index("col")

    def mine(array):
        return lax.dynamic_slice_in_dim(array, 2 * layer, 2, 0)

    my_rows, my_keep = mine(cheb_rows), mine(keep_mask)
    place, row_in, group = needs(my_rows, ham_cols, swap(ham_cols), row_group, layer, col)
    slots = jnp.broadcast_to(
        (2 * group[:, None, None] + jnp.arange(2, dtype=jnp.int32)[None, None, :]), (2, 2, 2)
    )
    keep_by_group = my_keep.reshape(2, 2, 2).transpose(1, 0, 2)
    keep = jnp.where(layer == 0, keep_by_group, keep_by_group[::-1])
    tables = (place.reshape(-1), row_in.reshape(-1), slots.reshape(-1), keep.reshape(-1))

    ham_pieces = []
    for blocks in (ham_blocks[:, 0], deriv_blocks[:, 0]):
        pieces = z_ring(blocks)
        flat = [pieces[z][0] for z in range(8) if z != 4] + pieces[4]
        ham_pieces += flat + [swap(piece) for piece in flat]

    def panel_of(cheb, tang):
        return lax.all_gather(jnp.stack([cheb, tang]), "row", axis=0)

    cheb, tang = mine(cheb_cur), mine(tang_cur)
    panel = panel_of(cheb, tang)
    cheb_mid, tang_mid = combine(tables, ham_pieces, panel, mine(cheb_prev), mine(tang_prev))
    panel = panel_of(cheb_mid, tang_mid)
    cheb_new, tang_new = combine(tables, ham_pieces, panel, cheb, tang)
    return (
        lax.all_gather(cheb_new, "depth", axis=0, tiled=True),
        lax.all_gather(tang_new, "depth", axis=0, tiled=True),
    )


def solution(mesh):
    placed = (
        P(("row", "depth"), "col", None, None),
        P(("row", "depth"), "col", None, None),
        P(("row", "depth"), None),
        P("col", "row", None, None),
        P("col", "row", None, None),
        P("col", "row", None, None),
        P("col", "row", None, None),
        P("col", None),
        P("col", "row"),
    )
    return jax.shard_map(
        on_device,
        mesh=mesh,
        in_specs=placed,
        out_specs=(P("col", "row", None, None), P("col", "row", None, None)),
        check_vma=False,
    )
```

```python
import functools

import jax
import jax.numpy as jnp
from jax import lax
from jax.experimental import pallas as pl
from jax.experimental.pallas import tpu as pltpu
from jax.sharding import PartitionSpec as P

ROWS, COLS, CORES = 16, 8, 2
SIDE = 4
CAP = 8
AXES = ("row", "col", "depth")
IOTA = functools.partial(jnp.arange, dtype=jnp.int32)
HBM = pl.BlockSpec(memory_space=pltpu.HBM)
VMEM = pl.BlockSpec(memory_space=pltpu.VMEM)
SMEM = pl.BlockSpec(memory_space=pltpu.SMEM)


def ring(shift):
    return [(i, (i + shift) % COLS) for i in range(COLS)]


def side_ring(shift, second):
    pairs = []
    for y in range(SIDE):
        for x in range(SIDE):
            for core in range(CORES):
                along_x = (core == 0) != second
                to_y = y if along_x else (y + shift) % SIDE
                to_x = (x + shift) % SIDE if along_x else x
                pairs.append(((y * SIDE + x) * CORES + core, (to_y * SIDE + to_x) * CORES + core))
    return pairs


def shift_side(array, shift, second):
    return lax.ppermute(array, ("row", "depth"), side_ring(shift, second))


def z_ring(blocks):
    half = blocks.shape[0] // 2
    up, down = [blocks], [blocks]
    for _ in range(3):
        up.append(lax.ppermute(up[-1], "col", ring(1)))
        down.append(lax.ppermute(down[-1], "col", ring(-1)))
    far_low = lax.ppermute(up[-1][:half], "col", ring(1))
    far_high = lax.ppermute(down[-1][half:], "col", ring(-1))
    near = [blocks, down[1], down[2], down[3], up[3], up[2], up[1]]
    return near + [far_low, far_high]


def swap(array):
    return lax.ppermute(array, "depth", [(0, 1), (1, 0)])


def combine_kernel(n_panels, table, *refs):
    ham, panels = refs[:36], refs[36 : 36 + n_panels]
    cheb_old, tang_old, cheb_new, tang_new, buf, acc, sems = refs[36 + n_panels :]

    def ham_copy(ref, row, slot, kind):
        return pltpu.make_async_copy(ref.at[row], buf.at[slot, kind], sems.at[slot, kind])

    def panel_copy(ref, piece, index, slot, kind):
        return pltpu.make_async_copy(
            ref.at[piece, kind, index], buf.at[slot, 2 + kind], sems.at[slot, 2 + kind]
        )

    def start_panel(place, slot):
        piece, index = lax.shift_right_logical(place, 3), place & 7
        for i, ref in enumerate(panels):

            def both(i=i, ref=ref):
                for kind in range(2):
                    panel_copy(ref, piece if n_panels == 1 else 0, index, slot, kind).start()

            if n_panels == 1:
                both()
            else:
                pl.when(piece == i)(both)

    def start_ham(owner, z, row, slot):
        def both(i, at):
            for kind in range(2):
                ham_copy(ham[(kind * 2 + owner) * 9 + i], at, slot, kind).start()

        if z == 4:
            pl.when(row < 8)(lambda: both(7, row))
            pl.when(row >= 8)(lambda: both(8, row - 8))
        else:
            both(z if z < 4 else z - 1, row)

    for owner in range(2):
        for z in range(COLS):

            def issue(i, carry, owner=owner, z=z):
                out = owner * 4 + i
                slot = out * COLS + z
                place = table[slot]

                @pl.when(place >= 0)
                def _():
                    start_ham(owner, z, table[64 + out], slot)
                    start_panel(place, slot)

                return carry

            lax.fori_loop(0, 4, issue, 0)

    acc[...] = jnp.zeros_like(acc)

    def work(slot, carry):
        @pl.when(table[slot] >= 0)
        def _():
            out = lax.shift_right_logical(slot, 3)
            for kind in range(2):
                ham_copy(ham[0], 0, slot, kind).wait()
                panel_copy(panels[0], 0, 0, slot, kind).wait()
            h, d, x, t = (buf[slot, i] for i in range(4))
            dot = functools.partial(jnp.dot, preferred_element_type=jnp.float32)
            acc[out, 0] += dot(h, x)
            acc[out, 1] += dot(d, x) + dot(h, t)

        return carry

    lax.fori_loop(0, 64, work, 0)

    def finish(out, carry):
        at = table[72 + out]
        scale = table[80 + out].astype(jnp.float32)
        old = cheb_old[at].astype(jnp.float32)
        cheb_new[at] = (scale * (2.0 * acc[out, 0] - old)).astype(jnp.bfloat16)
        old = tang_old[at].astype(jnp.float32)
        tang_new[at] = (scale * (2.0 * acc[out, 1] - old)).astype(jnp.bfloat16)
        return carry

    lax.fori_loop(0, 8, finish, 0)


def combine(table, ham_pieces, panels, cheb_old, tang_old):
    shape = jax.ShapeDtypeStruct(cheb_old.shape, jnp.bfloat16)
    return pl.pallas_call(
        functools.partial(combine_kernel, len(panels)),
        out_shape=(shape, shape),
        in_specs=[SMEM] + [HBM] * (36 + len(panels)) + [VMEM] * 2,
        out_specs=(VMEM, VMEM),
        scratch_shapes=[
            pltpu.VMEM((64, 4, 128, 128), jnp.bfloat16),
            pltpu.VMEM((8, 2, 128, 128), jnp.float32),
            pltpu.SemaphoreType.DMA((64, 4)),
        ],
        compiler_params=pltpu.CompilerParams(vmem_limit_bytes=24 * 1024 * 1024),
        cost_estimate=pl.CostEstimate(flops=1 << 30, bytes_accessed=1 << 23, transcendentals=0),
    )(table, *ham_pieces, *panels, cheb_old, tang_old)


def pack_kernel(table, *refs):
    panels, packed, sem = refs[:SIDE], refs[SIDE : SIDE + 3], refs[SIDE + 3]

    def copy(ref, index, out, i, slot):
        return pltpu.make_async_copy(ref.at[0, :, index], out.at[0, :, i], sem.at[slot])

    for wait in (False, True):
        for b, out in enumerate(packed):

            def step(i, carry, b=b, out=out, wait=wait):
                slot = b * CAP + i
                place = table[slot]

                @pl.when(place >= 0)
                def _():
                    if wait:
                        copy(panels[0], 0, out, i, slot).wait()
                    else:
                        for a, ref in enumerate(panels):

                            @pl.when(lax.shift_right_logical(place, 3) == a)
                            def _(ref=ref):
                                copy(ref, place & 7, out, i, slot).start()

                return carry

            lax.fori_loop(0, CAP, step, 0)


def pack(table, panels):
    shape = jax.ShapeDtypeStruct((1, 2, CAP, 128, 128), jnp.bfloat16)
    return pl.pallas_call(
        pack_kernel,
        out_shape=(shape,) * 3,
        in_specs=[SMEM] + [HBM] * SIDE,
        out_specs=(HBM,) * 3,
        scratch_shapes=[pltpu.SemaphoreType.DMA((3 * CAP,))],
        cost_estimate=pl.CostEstimate(flops=0, bytes_accessed=1 << 22, transcendentals=0),
    )(table, *panels)


def on_device(
    ham_blocks,
    deriv_blocks,
    ham_cols,
    cheb_prev,
    cheb_cur,
    tang_prev,
    tang_cur,
    cheb_rows,
    keep_mask,
):
    layer = lax.axis_index("depth")
    row_group = lax.axis_index("row")
    col = lax.axis_index("col")
    at_y, at_x = row_group // SIDE, row_group % SIDE
    first = jnp.where(layer == 0, at_x, at_y)
    second = jnp.where(layer == 0, at_y, at_x)

    def mine(array):
        return lax.dynamic_slice_in_dim(array, 2 * layer, 2, 0)

    my_rows = mine(cheb_rows)

    other_cols = swap(ham_cols)
    both_cols = jnp.where(layer == 0, jnp.stack([ham_cols, other_cols]), jnp.stack([other_cols, ham_cols]))
    known = jnp.concatenate([both_cols.reshape(32, 8), mine(keep_mask).reshape(1, 8)])
    known = jnp.stack([known] + [shift_side(known, SIDE - b, True) for b in (1, 2, 3)])
    cols_of = known[:, :32].reshape(4, 2, 16, 8)
    keep_of = known[:, 32].reshape(4, 2, 4)
    seconds = (second + IOTA(4)) % SIDE
    row_of = jnp.where(layer == 0, seconds * SIDE + first, first * SIDE + seconds)
    wanted = jnp.arange(16, dtype=jnp.int32)[None, :, None] == row_of[:, None, None]
    rows = jnp.sum(jnp.where(wanted[:, None], my_rows.reshape(1, 2, 16, 4), 0), axis=2)
    row_in = rows - row_of[:, None, None] * 32 - 16 * (IOTA(4) // 2)
    onehot = row_in[..., None] == IOTA(16)
    cols_t = jnp.stack([cols_of[:, 0], cols_of[:, 0], cols_of[:, 1], cols_of[:, 1]], axis=1)
    needed = jnp.sum(jnp.where(onehot[..., None], cols_t[:, None], 0), axis=3)
    equal = needed[..., None] == my_rows[None, :, None, None, :]
    equal = equal & (keep_of[..., None, None] != 0)
    place = jnp.max(jnp.where(equal, IOTA(64), -1), axis=-1).reshape(4, 64)
    column = IOTA(64) // 32
    from_row = place // 4
    from_first = jnp.where(layer == 0, from_row % SIDE, from_row // SIDE)
    from_second = jnp.where(layer == 0, from_row // SIDE, from_row % SIDE)
    index = column * 4 + place % 4
    near = ((from_first - first) % SIDE) * 8 + index

    def ranks(mask):
        before = IOTA(64)[:, None] > IOTA(64)[None, :]
        return jnp.sum(jnp.where(before & mask[:, None, :], 1, 0), axis=-1)

    send = (place >= 0) & (from_second == second)
    rank = ranks(send)
    chosen = send[:, None, :] & (rank[:, None, :] == IOTA(CAP)[:, None])
    pack_table = jnp.max(jnp.where(chosen, near[:, None, :], -1), axis=-1)[1:].reshape(-1)

    behind = (second - from_second[0]) % SIDE
    take = (place[:1] >= 0) & (behind[None] == IOTA(4)[:, None])
    take_rank = jnp.sum(jnp.where(take, ranks(take), 0), axis=0)
    sparse_place = jnp.where(behind == 0, near[0], (behind + 3) * 8 + take_rank)
    sparse_place = jnp.where(place[0] >= 0, sparse_place, -1)
    dense_place = jnp.where(place[0] >= 0, from_row[0] * 8 + index[0], -1)
    count = jnp.sum(jnp.where(take, 1, 0), axis=-1)
    overflow = jnp.any(count[1:] > CAP).astype(jnp.int32)
    flags = lax.all_to_all(jnp.broadcast_to(overflow, (256, 1, 128)), AXES, 0, 0, tiled=True)
    crowded = jnp.max(flags) > 0

    def by_owner(array):
        array = array.reshape((2, 2, 2) + array.shape[2:]).swapaxes(0, 1)
        return jnp.where(layer == 0, array, array[::-1])

    order = (col + IOTA(8)) % 8
    turn = order[:, None] == IOTA(8)

    def kernel_table(places):
        places = jnp.sum(jnp.where(turn, places.reshape(2, 4, 1, 8), 0), axis=-1)
        parts = (places, row_in[0], IOTA(8).reshape(2, 4), keep_of[0])
        return jnp.concatenate([by_owner(part).reshape(-1) for part in parts])

    dense_table, sparse_table = kernel_table(dense_place), kernel_table(sparse_place)

    ham_pieces = []
    for blocks in (ham_blocks[:, 0], deriv_blocks[:, 0]):
        pieces = z_ring(blocks)
        ham_pieces += pieces + [swap(piece) for piece in pieces]

    def own(array):
        return mine(array).reshape(8, 128, 128)

    def dense(cheb, tang):
        return lax.all_gather(jnp.stack([cheb, tang]), "row", axis=0)

    def sparse_step(ham_pieces, cheb, tang, cheb_old, tang_old):
        piece = jnp.stack([cheb, tang])[None]
        near_pieces = [piece] + [shift_side(piece, SIDE - a, False) for a in (1, 2, 3)]
        packed = pack(pack_table, near_pieces)
        arrived = [shift_side(packed[b - 1], b, True) for b in (1, 2, 3)]
        return combine(sparse_table, ham_pieces, near_pieces + arrived, cheb_old, tang_old)

    def dense_step(ham_pieces, cheb, tang, cheb_old, tang_old):
        return combine(dense_table, ham_pieces, [dense(cheb, tang)], cheb_old, tang_old)

    cheb, tang = own(cheb_cur), own(tang_cur)
    cheb_mid, tang_mid = dense_step(ham_pieces, cheb, tang, own(cheb_prev), own(tang_prev))
    cheb_new, tang_new = lax.cond(
        crowded, dense_step, sparse_step, ham_pieces, cheb_mid, tang_mid, cheb, tang
    )

    def whole(array):
        return lax.all_gather(array.reshape(2, 4, 128, 128), "depth", axis=0, tiled=True)

    return whole(cheb_new), whole(tang_new)


def solution(mesh):
    placed = (
        P(("row", "depth"), "col", None, None),
        P(("row", "depth"), "col", None, None),
        P(("row", "depth"), None),
        P("col", "row", None, None),
        P("col", "row", None, None),
        P("col", "row", None, None),
        P("col", "row", None, None),
        P("col", None),
        P("col", "row"),
    )
    return jax.shard_map(
        on_device,
        mesh=mesh,
        in_specs=placed,
        out_specs=(P("col", "row", None, None), P("col", "row", None, None)),
        check_vma=False,
    )
```

```python
import functools

import jax
import jax.numpy as jnp
from jax import lax
from jax.experimental import pallas as pl
from jax.experimental.pallas import tpu as pltpu
from jax.sharding import PartitionSpec as P

ROWS, COLS, CORES = 16, 8, 2
SIDE = 4
CAP = 8
AXES = ("row", "col", "depth")
IOTA = functools.partial(jnp.arange, dtype=jnp.int32)
HBM = pl.BlockSpec(memory_space=pltpu.HBM)
VMEM = pl.BlockSpec(memory_space=pltpu.VMEM)
SMEM = pl.BlockSpec(memory_space=pltpu.SMEM)
ROW_AT, PLACE_AT, OUT_AT, KEEP_AT = 40, 104, 168, 232


def ring(shift):
    return [(i, (i + shift) % COLS) for i in range(COLS)]


def side_ring(shift, second):
    pairs = []
    for y in range(SIDE):
        for x in range(SIDE):
            for core in range(CORES):
                along_x = (core == 0) != second
                to_y = y if along_x else (y + shift) % SIDE
                to_x = (x + shift) % SIDE if along_x else x
                pairs.append(((y * SIDE + x) * CORES + core, (to_y * SIDE + to_x) * CORES + core))
    return pairs


def shift_side(array, shift, second):
    return lax.ppermute(array, ("row", "depth"), side_ring(shift, second))


def z_ring(halves):
    ups, downs = [[half] for half in halves], [[half] for half in halves]
    for _ in range(3):
        for up, down in zip(ups, downs, strict=True):
            up.append(lax.ppermute(up[-1], "col", ring(1)))
            down.append(lax.ppermute(down[-1], "col", ring(-1)))

    def last(ready):
        low, high, ready = lax.optimization_barrier((ups[0][3], downs[1][3], ready))
        far = [lax.ppermute(low, "col", ring(1)), lax.ppermute(high, "col", ring(-1))]
        near = [[halves[0], halves[1]]] + [[down[i] for down in downs] for i in (1, 2, 3)]
        return near + [far] + [[up[i] for up in ups] for i in (3, 2, 1)], ready

    return ups[0][1], last


def swap(array):
    return lax.ppermute(array, "depth", [(0, 1), (1, 0)])


def combine_kernel(n_panels, table, *refs):
    ham, panels = refs[:32], refs[32 : 32 + n_panels]
    cheb_old, tang_old, cheb_new, tang_new, ham_buf, panel_buf, acc, sems = refs[32 + n_panels :]

    def start_panel(place, chunk, i):
        def copy(ref, index):
            pltpu.make_async_copy(ref.at[index], panel_buf.at[chunk, i], sems.at[1, chunk]).start()

        if n_panels == 1:
            copy(panels[0], place)
        else:
            piece = lax.shift_right_logical(place, 3)
            for k, ref in enumerate(panels):
                pl.when(piece == k)(functools.partial(copy, ref, place & 7))

    for k, ref in enumerate(ham):

        def issue(entry, carry, ref=ref):
            chunk, i = lax.shift_right_logical(entry, 2), entry & 3
            row = table[ROW_AT + entry]
            pltpu.make_async_copy(ref.at[row], ham_buf.at[chunk, i], sems.at[0, chunk]).start()
            start_panel(table[PLACE_AT + entry], chunk, i)
            return carry

        lax.fori_loop(table[k], table[k + 1], issue, 0)

    acc[...] = jnp.zeros_like(acc)
    zero = jnp.zeros((128, 128), jnp.bfloat16)

    def work(chunk, carry):
        pltpu.make_async_copy(ham_buf.at[chunk], ham_buf.at[chunk], sems.at[0, chunk]).wait()
        pltpu.make_async_copy(panel_buf.at[chunk], panel_buf.at[chunk], sems.at[1, chunk]).wait()
        sums = []
        for i in range(4):
            x, t = panel_buf[chunk, i, 0], panel_buf[chunk, i, 1]
            left = jnp.concatenate([ham_buf[chunk, i, 0], ham_buf[chunk, i, 1]], axis=1)
            top = jnp.concatenate([x, t], axis=1)
            right = jnp.concatenate([top, jnp.concatenate([zero, x], axis=1)], axis=0)
            sums.append(jnp.dot(left, right, preferred_element_type=jnp.float32))
        for i in range(4):
            acc[table[OUT_AT + chunk * 4 + i]] += sums[i]
        return carry

    lax.fori_loop(0, lax.shift_right_logical(table[32], 2), work, 0)

    for out in range(8):
        scale = table[KEEP_AT + out].astype(jnp.float32)
        old = cheb_old[out].astype(jnp.float32)
        cheb_new[out] = (scale * (2.0 * acc[out, :, :128] - old)).astype(jnp.bfloat16)
        old = tang_old[out].astype(jnp.float32)
        tang_new[out] = (scale * (2.0 * acc[out, :, 128:] - old)).astype(jnp.bfloat16)


def combine(table, ham_pieces, panels, cheb_old, tang_old):
    shape = jax.ShapeDtypeStruct(cheb_old.shape, jnp.bfloat16)
    return pl.pallas_call(
        functools.partial(combine_kernel, len(panels)),
        out_shape=(shape, shape),
        in_specs=[SMEM] + [HBM] * (32 + len(panels)) + [VMEM] * 2,
        out_specs=(VMEM, VMEM),
        scratch_shapes=[
            pltpu.VMEM((16, 4, 2, 128, 128), jnp.bfloat16),
            pltpu.VMEM((16, 4, 2, 128, 128), jnp.bfloat16),
            pltpu.VMEM((9, 128, 256), jnp.float32),
            pltpu.SemaphoreType.DMA((2, 16)),
        ],
        compiler_params=pltpu.CompilerParams(vmem_limit_bytes=24 * 1024 * 1024),
        cost_estimate=pl.CostEstimate(flops=1 << 30, bytes_accessed=1 << 23, transcendentals=0),
    )(table, *ham_pieces, *panels, cheb_old, tang_old)


def pack_kernel(table, *refs):
    panels, packed, sem = refs[:SIDE], refs[SIDE : SIDE + 3], refs[SIDE + 3]

    def copy(ref, index, out, i, slot):
        return pltpu.make_async_copy(ref.at[index], out.at[i], sem.at[slot])

    for wait in (False, True):
        for b, out in enumerate(packed):

            def step(i, carry, b=b, out=out, wait=wait):
                slot = b * CAP + i
                place = table[slot]
                if wait:
                    copy(panels[0], 0, out, i, slot).wait()
                else:
                    for a, ref in enumerate(panels):

                        @pl.when(lax.shift_right_logical(place, 3) == a)
                        def _(ref=ref):
                            copy(ref, place & 7, out, i, slot).start()

                return carry

            lax.fori_loop(0, table[3 * CAP + b], step, 0)


def pack(table, panels):
    shape = jax.ShapeDtypeStruct((CAP, 2, 128, 128), jnp.bfloat16)
    return pl.pallas_call(
        pack_kernel,
        out_shape=(shape,) * 3,
        in_specs=[SMEM] + [HBM] * SIDE,
        out_specs=(VMEM,) * 3,
        scratch_shapes=[pltpu.SemaphoreType.DMA((3 * CAP,))],
        cost_estimate=pl.CostEstimate(flops=0, bytes_accessed=1 << 22, transcendentals=0),
    )(table, *panels)


def on_device(
    ham_blocks,
    deriv_blocks,
    ham_cols,
    cheb_prev,
    cheb_cur,
    tang_prev,
    tang_cur,
    cheb_rows,
    keep_mask,
):
    layer = lax.axis_index("depth")
    row_group = lax.axis_index("row")
    col = lax.axis_index("col")
    at_y, at_x = row_group // SIDE, row_group % SIDE
    first = jnp.where(layer == 0, at_x, at_y)
    second = jnp.where(layer == 0, at_y, at_x)

    def mine(array):
        return lax.dynamic_slice_in_dim(array, 2 * layer, 2, 0)

    my_rows = mine(cheb_rows)

    def own(array):
        return mine(array).reshape(8, 128, 128)

    def paired(cheb, tang):
        return jnp.stack([cheb, tang], axis=1)

    cheb, tang = own(cheb_cur), own(tang_cur)
    ham_pair = jnp.stack([ham_blocks[:, 0], deriv_blocks[:, 0]], axis=1)
    first_arrival, last_step = z_ring([ham_pair[:8], ham_pair[8:]])
    ham_cols, _ = lax.optimization_barrier((ham_cols, first_arrival))

    other_cols = swap(ham_cols)
    both_cols = jnp.where(layer == 0, jnp.stack([ham_cols, other_cols]), jnp.stack([other_cols, ham_cols]))
    known = jnp.concatenate([both_cols.reshape(32, 8), mine(keep_mask).reshape(1, 8)])
    known = jnp.stack([known] + [shift_side(known, SIDE - b, True) for b in (1, 2, 3)])
    cols_of = known[:, :32].reshape(4, 2, 16, 8)
    keep_of = known[:, 32].reshape(4, 2, 4)
    seconds = (second + IOTA(4)) % SIDE
    row_of = jnp.where(layer == 0, seconds * SIDE + first, first * SIDE + seconds)
    wanted = jnp.arange(16, dtype=jnp.int32)[None, :, None] == row_of[:, None, None]
    rows = jnp.sum(jnp.where(wanted[:, None], my_rows.reshape(1, 2, 16, 4), 0), axis=2)
    row_in = rows - row_of[:, None, None] * 32 - 16 * (IOTA(4) // 2)
    onehot = row_in[..., None] == IOTA(16)
    cols_t = jnp.stack([cols_of[:, 0], cols_of[:, 0], cols_of[:, 1], cols_of[:, 1]], axis=1)
    needed = jnp.sum(jnp.where(onehot[..., None], cols_t[:, None], 0), axis=3)
    equal = needed[..., None] == my_rows[None, :, None, None, :]
    equal = equal & (keep_of[..., None, None] != 0)
    place = jnp.max(jnp.where(equal, IOTA(64), -1), axis=-1).reshape(4, 64)
    column = IOTA(64) // 32
    from_row = place // 4
    from_first = jnp.where(layer == 0, from_row % SIDE, from_row // SIDE)
    from_second = jnp.where(layer == 0, from_row // SIDE, from_row % SIDE)
    index = column * 4 + place % 4
    near = ((from_first - first) % SIDE) * 8 + index

    def ranks(mask):
        before = IOTA(64)[:, None] > IOTA(64)[None, :]
        return jnp.sum(jnp.where(before & mask[:, None, :], 1, 0), axis=-1)

    send = (place >= 0) & (from_second == second)
    rank = ranks(send)
    chosen = send[:, None, :] & (rank[:, None, :] == IOTA(CAP)[:, None])
    pack_table = jnp.max(jnp.where(chosen, near[:, None, :], -1), axis=-1)[1:].reshape(-1)
    sent = jnp.minimum(jnp.sum(jnp.where(send, 1, 0), axis=-1), CAP)[1:]
    pack_table = jnp.concatenate([pack_table, sent])

    behind = (second - from_second[0]) % SIDE
    take = (place[:1] >= 0) & (behind[None] == IOTA(4)[:, None])
    take_rank = jnp.sum(jnp.where(take, ranks(take), 0), axis=0)
    sparse_place = jnp.where(behind == 0, near[0], (behind + 3) * 8 + take_rank)
    sparse_place = jnp.where(place[0] >= 0, sparse_place, -1)
    dense_place = jnp.where(place[0] >= 0, from_row[0] * 8 + index[0], -1)
    count = jnp.sum(jnp.where(take, 1, 0), axis=-1)
    overflow = jnp.any(count[1:] > CAP).astype(jnp.int32)
    flags = lax.all_to_all(jnp.broadcast_to(overflow, (256, 1, 128)), AXES, 0, 0, tiled=True)
    crowded = jnp.max(flags) > 0

    found = place[0] >= 0
    entry_out = IOTA(64) // 8
    owner = (entry_out % 4 // 2 + layer) % 2
    offset = (IOTA(8)[None, :] - col) % 8 + jnp.zeros((8, 1), jnp.int32)
    row64 = jnp.broadcast_to(row_in[0].reshape(8, 1), (8, 8)).reshape(64)
    group = owner * 16 + offset.reshape(64) * 2 + row64 // 8
    key = group * 64 + IOTA(64)
    position = jnp.sum(jnp.where(found[None, :] & (key[None, :] < key[:, None]), 1, 0), axis=1)
    total = jnp.sum(jnp.where(found, 1, 0))
    bounds = jnp.sum(jnp.where(found[None, :] & (group[None, :] < IOTA(40)[:, None]), 1, 0), axis=1)
    bounds = jnp.where(IOTA(40) >= 32, (total + 3) // 4 * 4, bounds)
    here = found[None, :] & (position[None, :] == IOTA(64)[:, None])

    def listed(values, empty):
        return jnp.where(IOTA(64) < total, jnp.sum(jnp.where(here, values[None, :], 0), axis=1), empty)

    def kernel_table(places):
        parts = (listed(row64 % 8, 0), listed(places, 0), listed(entry_out, 8), keep_of[0].reshape(8))
        return jnp.concatenate((bounds,) + parts)

    dense_table, sparse_table = kernel_table(dense_place), kernel_table(sparse_place)

    pieces, (dense_table, sparse_table, pack_table, crowded) = last_step(
        (dense_table, sparse_table, pack_table, crowded)
    )
    flat = [half for piece in pieces for half in piece]
    ham_pieces = flat + [swap(half) for half in flat]

    def sparse_step(ham_pieces, cheb, tang, cheb_old, tang_old):
        piece = paired(cheb, tang)
        near_pieces = [piece] + [shift_side(piece, SIDE - a, False) for a in (1, 2, 3)]
        packed = pack(pack_table, near_pieces)
        arrived = [shift_side(packed[b - 1], b, True) for b in (1, 2, 3)]
        return combine(sparse_table, ham_pieces, near_pieces + arrived, cheb_old, tang_old)

    def dense_step(ham_pieces, cheb, tang, cheb_old, tang_old):
        panel = lax.all_gather(paired(cheb, tang), "row", axis=0, tiled=True)
        return combine(dense_table, ham_pieces, [panel], cheb_old, tang_old)

    cheb_mid, tang_mid = dense_step(ham_pieces, cheb, tang, own(cheb_prev), own(tang_prev))
    cheb_new, tang_new = lax.cond(
        crowded, dense_step, sparse_step, ham_pieces, cheb_mid, tang_mid, cheb, tang
    )

    def whole(array):
        other = swap(array)
        both = jnp.stack([jnp.where(layer == 0, array, other), jnp.where(layer == 0, other, array)])
        return both.reshape(4, 4, 128, 128)

    return whole(cheb_new), whole(tang_new)


def solution(mesh):
    placed = (
        P(("row", "depth"), "col", None, None),
        P(("row", "depth"), "col", None, None),
        P(("row", "depth"), None),
        P("col", "row", None, None),
        P("col", "row", None, None),
        P("col", "row", None, None),
        P("col", "row", None, None),
        P("col", None),
        P("col", "row"),
    )
    return jax.shard_map(
        on_device,
        mesh=mesh,
        in_specs=placed,
        out_specs=(P("col", "row", None, None), P("col", "row", None, None)),
        check_vma=False,
    )
```

```python
import functools

import jax
import jax.numpy as jnp
from jax import lax
from jax.experimental import pallas as pl
from jax.experimental.pallas import tpu as pltpu
from jax.sharding import PartitionSpec as P

ROWS, COLS, CORES = 16, 8, 2
SIDE = 4
CAP = 8
AXES = ("row", "col", "depth")
HBM = pl.BlockSpec(memory_space=pltpu.HBM)
VMEM = pl.BlockSpec(memory_space=pltpu.VMEM)
SMEM = pl.BlockSpec(memory_space=pltpu.SMEM)
ANY = pl.BlockSpec(memory_space=pl.ANY)
HAM_AT, PLACE_AT, OUT_AT, KEEP_AT, COUNT_AT = 0, 64, 128, 192, 200


def side_ring(shift, second):
    pairs = []
    for y in range(SIDE):
        for x in range(SIDE):
            for core in range(CORES):
                along_x = (core == 0) != second
                to_y = y if along_x else (y + shift) % SIDE
                to_x = (x + shift) % SIDE if along_x else x
                pairs.append(((y * SIDE + x) * CORES + core, (to_y * SIDE + to_x) * CORES + core))
    return pairs


def shift_side(array, shift, second):
    return lax.ppermute(array, ("row", "depth"), side_ring(shift, second))


def swap(array):
    return lax.ppermute(array, "depth", [(0, 1), (1, 0)])


def combine_kernel(n_panels, table, ham, *refs):
    panels = refs[:n_panels]
    cheb_old, tang_old, cheb_new, tang_new, ham_buf, panel_buf, acc, sems = refs[n_panels:]

    def issue(entry, carry):
        chunk, i = lax.shift_right_logical(entry, 2), entry & 3
        source = ham.at[table[HAM_AT + entry]]
        pltpu.make_async_copy(source, ham_buf.at[chunk, i], sems.at[0, chunk]).start()
        place = table[PLACE_AT + entry]

        def copy(ref, index):
            pltpu.make_async_copy(ref.at[index], panel_buf.at[chunk, i], sems.at[1, chunk]).start()

        if n_panels == 1:
            copy(panels[0], place)
        else:
            for k, ref in enumerate(panels):
                pl.when(lax.shift_right_logical(place, 3) == k)(functools.partial(copy, ref, place & 7))
        return carry

    lax.fori_loop(0, table[COUNT_AT], issue, 0)
    acc[...] = jnp.zeros_like(acc)
    zero = jnp.zeros((128, 128), jnp.bfloat16)

    def work(chunk, carry):
        pltpu.make_async_copy(ham_buf.at[chunk], ham_buf.at[chunk], sems.at[0, chunk]).wait()
        pltpu.make_async_copy(panel_buf.at[chunk], panel_buf.at[chunk], sems.at[1, chunk]).wait()
        sums = []
        for i in range(4):
            x, t = panel_buf[chunk, i, 0], panel_buf[chunk, i, 1]
            left = jnp.concatenate([ham_buf[chunk, i, 0], ham_buf[chunk, i, 1]], axis=1)
            top = jnp.concatenate([x, t], axis=1)
            right = jnp.concatenate([top, jnp.concatenate([zero, x], axis=1)], axis=0)
            sums.append(jnp.dot(left, right, preferred_element_type=jnp.float32))
        for i in range(4):
            acc[table[OUT_AT + chunk * 4 + i]] += sums[i]
        return carry

    lax.fori_loop(0, lax.shift_right_logical(table[COUNT_AT], 2), work, 0)

    for out in range(8):
        scale = table[KEEP_AT + out].astype(jnp.float32)
        old = cheb_old[out].astype(jnp.float32)
        cheb_new[out] = (scale * (2.0 * acc[out, :, :128] - old)).astype(jnp.bfloat16)
        old = tang_old[out].astype(jnp.float32)
        tang_new[out] = (scale * (2.0 * acc[out, :, 128:] - old)).astype(jnp.bfloat16)


def combine(table, ham, panels, cheb_old, tang_old):
    shape = jax.ShapeDtypeStruct(cheb_old.shape, jnp.bfloat16)
    return pl.pallas_call(
        functools.partial(combine_kernel, len(panels)),
        out_shape=(shape, shape),
        in_specs=[SMEM, HBM] + [ANY] * len(panels) + [VMEM] * 2,
        out_specs=(VMEM, VMEM),
        scratch_shapes=[
            pltpu.VMEM((16, 4, 2, 128, 128), jnp.bfloat16),
            pltpu.VMEM((16, 4, 2, 128, 128), jnp.bfloat16),
            pltpu.VMEM((9, 128, 256), jnp.float32),
            pltpu.SemaphoreType.DMA((2, 16)),
        ],
        compiler_params=pltpu.CompilerParams(vmem_limit_bytes=24 * 1024 * 1024),
        cost_estimate=pl.CostEstimate(flops=1 << 30, bytes_accessed=1 << 23, transcendentals=0),
    )(table, ham, *panels, cheb_old, tang_old)


def pack_kernel(table, *refs):
    panels, packed, sem = refs[:SIDE], refs[SIDE : SIDE + 3], refs[SIDE + 3]

    def copy(ref, index, out, i, slot):
        return pltpu.make_async_copy(ref.at[index], out.at[i], sem.at[slot])

    for wait in (False, True):
        for b, out in enumerate(packed):

            def step(i, carry, b=b, out=out, wait=wait):
                slot = b * CAP + i
                place = table[slot]
                if wait:
                    copy(panels[0], 0, out, i, slot).wait()
                else:
                    for a, ref in enumerate(panels):

                        @pl.when(lax.shift_right_logical(place, 3) == a)
                        def _(ref=ref):
                            copy(ref, place & 7, out, i, slot).start()

                return carry

            lax.fori_loop(0, table[3 * CAP + b], step, 0)


def pack(table, panels):
    shape = jax.ShapeDtypeStruct((CAP, 2, 128, 128), jnp.bfloat16)
    return pl.pallas_call(
        pack_kernel,
        out_shape=(shape,) * 3,
        in_specs=[SMEM] + [ANY] * SIDE,
        out_specs=(VMEM,) * 3,
        scratch_shapes=[pltpu.SemaphoreType.DMA((3 * CAP,))],
        cost_estimate=pl.CostEstimate(flops=0, bytes_accessed=1 << 22, transcendentals=0),
    )(table, *panels)


def position():
    layer, row_group, col = (lax.axis_index(name) for name in ("depth", "row", "col"))
    at_y, at_x = lax.shift_right_logical(row_group, 2), row_group & 3
    return layer, row_group, col, jnp.where(layer == 0, at_x, at_y), jnp.where(layer == 0, at_y, at_x)


def slots_of_rows(rows, layer, slot_of):
    def fill(slot, carry):
        for column in range(2):
            slot_of[column * 512 + rows[2 * layer + column, slot]] = slot
        return carry

    lax.fori_loop(0, 64, fill, 0)


def split(i):
    return lax.shift_right_logical(i, 5), lax.shift_right_logical(i, 3) & 3, i & 7


def coordinates(slot, layer):
    y, x = lax.shift_right_logical(slot, 4), lax.shift_right_logical(slot, 2) & 3
    return jnp.where(layer == 0, x, y), jnp.where(layer == 0, y, x)


def needs_kernel(rows, cols, other_cols, keep, *refs):
    tables, flag, slot_of, counts = refs[:3], refs[3], refs[4], refs[5]
    layer, row_group, col, first, second = position()
    slots_of_rows(rows, layer, slot_of)
    for i in range(5):
        counts[i] = 0

    def put(at, ham, out, places):
        for table, place in zip(tables, places, strict=True):
            table[HAM_AT + at] = ham
            table[OUT_AT + at] = out
            table[PLACE_AT + at] = place

    def look(i, carry):
        column, t, q = split(i)
        group = lax.shift_right_logical(t, 1)
        row = rows[2 * layer + column, 4 * row_group + t] - 32 * row_group - 16 * group
        wanted = jnp.where(group == layer, cols[row, q], other_cols[row, q])
        slot = slot_of[column * 512 + wanted] & 63

        @pl.when((rows[2 * layer + column, slot] == wanted) & (keep[2 * layer + column, t] != 0))
        def _():
            at_first, at_second = coordinates(slot, layer)
            sender = (second - at_second) & 3
            rank = counts[sender]
            counts[sender] = rank + 1
            index = column * 4 + (slot & 3)
            near = ((at_first - first) & 3) * 8 + index
            n = counts[4]
            counts[4] = n + 1
            sparse = jnp.where(sender == 0, near, (sender + 3) * 8 + rank)
            places = (((4 - sender) & 3) * 32 + near, sparse, lax.shift_right_logical(slot, 2) * 8 + index)
            put(n, (q * 2 + group) * 16 + row, lax.shift_right_logical(i, 3), places)

        return carry

    lax.fori_loop(0, 64, look, 0)
    flag[0] = jnp.where((counts[1] > CAP) | (counts[2] > CAP) | (counts[3] > CAP), 1, 0)
    n = counts[4]
    padded = (n + 3) & ~3

    def pad(i, carry):
        put(i, 0, 8, (0, 0, 0))
        return carry

    lax.fori_loop(n, padded, pad, 0)
    for table in tables:
        table[COUNT_AT] = padded
        for out in range(8):
            table[KEEP_AT + out] = keep[2 * layer + out // 4, out % 4]


def needs(cheb_rows, ham_cols, other_cols, keep_mask):
    table = jax.ShapeDtypeStruct((208,), jnp.int32)
    return pl.pallas_call(
        needs_kernel,
        out_shape=(table,) * 3 + (jax.ShapeDtypeStruct((1,), jnp.int32),),
        in_specs=[SMEM] * 4,
        out_specs=(SMEM,) * 4,
        scratch_shapes=[pltpu.SMEM((size,), jnp.int32) for size in (1024, 8)],
    )(cheb_rows, ham_cols, other_cols, keep_mask)


def sends_kernel(rows, *refs):
    known, (table, slot_of, count) = refs[:3], refs[3:]
    layer, row_group, col, first, second = position()
    slots_of_rows(rows, layer, slot_of)
    for b, theirs in enumerate(known):
        to_second = (second + 1 + b) & 3
        to_row = jnp.where(layer == 0, to_second * SIDE + first, first * SIDE + to_second)
        count[0] = 0

        def look(i, carry, b=b, theirs=theirs, to_row=to_row):
            column, t, q = split(i)
            group = lax.shift_right_logical(t, 1)
            row = rows[2 * layer + column, 4 * to_row + t] - 32 * to_row - 16 * group
            wanted = theirs[jnp.where(group == layer, 0, 16) + row, q]
            slot = slot_of[column * 512 + wanted] & 63
            at = (2 * layer + column) * 4 + t
            kept = theirs[32 + lax.shift_right_logical(at, 3), at & 7] != 0
            at_first, at_second = coordinates(slot, layer)

            @pl.when((rows[2 * layer + column, slot] == wanted) & kept & (at_second == second))
            def _():
                rank = count[0]
                count[0] = rank + 1

                @pl.when(rank < CAP)
                def _():
                    table[b * CAP + rank] = ((at_first - first) & 3) * 8 + column * 4 + (slot & 3)

            return carry

        lax.fori_loop(0, 64, look, 0)
        table[3 * CAP + b] = jnp.minimum(count[0], CAP)


def sends(cheb_rows, known):
    return pl.pallas_call(
        sends_kernel,
        out_shape=jax.ShapeDtypeStruct((32,), jnp.int32),
        in_specs=[SMEM] * 4,
        out_specs=SMEM,
        scratch_shapes=[pltpu.SMEM((1024,), jnp.int32), pltpu.SMEM((1,), jnp.int32)],
    )(cheb_rows, *known)


def on_device(
    ham_blocks,
    deriv_blocks,
    ham_cols,
    cheb_prev,
    cheb_cur,
    tang_prev,
    tang_cur,
    cheb_rows,
    keep_mask,
):
    layer = lax.axis_index("depth")

    def mine(array):
        return lax.dynamic_slice_in_dim(array, 2 * layer, 2, 0)

    def own(array):
        return mine(array).reshape(8, 128, 128)

    def paired(cheb, tang):
        return jnp.stack([cheb, tang], axis=1)

    cheb, tang = own(cheb_cur), own(tang_cur)
    ham_pair = jnp.stack([ham_blocks[:, 0], deriv_blocks[:, 0]], axis=1)
    ham = lax.all_gather(ham_pair, ("col", "depth"), axis=0, tiled=True)

    other_cols = swap(ham_cols)
    ring_table, sparse_table, dense_table, overflow = needs(cheb_rows, ham_cols, other_cols, keep_mask)
    flags = lax.all_to_all(jnp.broadcast_to(overflow, (256, 1, 128)), AXES, 0, 0, tiled=True)
    known = jnp.concatenate([ham_cols, other_cols, keep_mask.reshape(2, 8)])
    pack_table = sends(cheb_rows, [shift_side(known, SIDE - b, True) for b in (1, 2, 3)])

    def nearby(piece):
        return [piece] + [shift_side(piece, SIDE - a, False) for a in (1, 2, 3)]

    def ring_panel(piece, ready):
        here = nearby(piece)
        after = [shift_side(piece, SIDE - 1, True) for piece in here]
        before = [shift_side(piece, 1, True) for piece in here]
        last, ready = lax.optimization_barrier((after[0], ready))
        across = [shift_side(piece, SIDE - 1, True) for piece in (last, after[1])]
        across += [shift_side(piece, 1, True) for piece in before[2:]]
        return here + after + across + before, ready

    def sparse_step(ham, cheb, tang, cheb_old, tang_old):
        near_pieces = nearby(paired(cheb, tang))
        packed = pack(pack_table, near_pieces)
        arrived = [shift_side(packed[b - 1], b, True) for b in (1, 2, 3)]
        return combine(sparse_table, ham, near_pieces + arrived, cheb_old, tang_old)

    def dense_step(ham, cheb, tang, cheb_old, tang_old):
        panel = lax.all_gather(paired(cheb, tang), "row", axis=0, tiled=True)
        return combine(dense_table, ham, [panel], cheb_old, tang_old)

    panel, (flags, pack_table) = ring_panel(paired(cheb, tang), (flags, pack_table))
    crowded = jnp.max(flags) > 0
    cheb_mid, tang_mid = combine(ring_table, ham, panel, own(cheb_prev), own(tang_prev))
    cheb_new, tang_new = lax.cond(crowded, dense_step, sparse_step, ham, cheb_mid, tang_mid, cheb, tang)

    def whole(array):
        other = swap(array)
        both = jnp.stack([jnp.where(layer == 0, array, other), jnp.where(layer == 0, other, array)])
        return both.reshape(4, 4, 128, 128)

    return whole(cheb_new), whole(tang_new)


def solution(mesh):
    placed = (
        P(("row", "depth"), "col", None, None),
        P(("row", "depth"), "col", None, None),
        P(("row", "depth"), None),
        P("col", "row", None, None),
        P("col", "row", None, None),
        P("col", "row", None, None),
        P("col", "row", None, None),
        P("col", None),
        P("col", "row"),
    )
    return jax.shard_map(
        on_device,
        mesh=mesh,
        in_specs=placed,
        out_specs=(P("col", "row", None, None), P("col", "row", None, None)),
        check_vma=False,
    )
```

```python
import functools

import jax
import jax.numpy as jnp
from jax import lax
from jax.experimental import pallas as pl
from jax.experimental.pallas import tpu as pltpu
from jax.sharding import PartitionSpec as P

ROWS, COLS, CORES = 16, 8, 2
SIDE = 4
CAP = 8
VMEM_BYTES = 56 * 1024 * 1024
AXES = ("row", "col", "depth")
HBM = pl.BlockSpec(memory_space=pltpu.HBM)
VMEM = pl.BlockSpec(memory_space=pltpu.VMEM)
SMEM = pl.BlockSpec(memory_space=pltpu.SMEM)
ANY = pl.BlockSpec(memory_space=pl.ANY)
HAM_AT, PLACE_AT, OUT_AT, KEEP_AT, COUNT_AT = 0, 64, 128, 192, 200


def side_ring(shift, second):
    pairs = []
    for y in range(SIDE):
        for x in range(SIDE):
            for core in range(CORES):
                along_x = (core == 0) != second
                to_y = y if along_x else (y + shift) % SIDE
                to_x = (x + shift) % SIDE if along_x else x
                pairs.append(((y * SIDE + x) * CORES + core, (to_y * SIDE + to_x) * CORES + core))
    return pairs


def shift_side(array, shift, second):
    return lax.ppermute(array, ("row", "depth"), side_ring(shift, second))


def swap(array):
    return lax.ppermute(array, "depth", [(0, 1), (1, 0)])


def combine_kernel(n_panels, apart, table, ham, *refs):
    panels, old, new = refs[:n_panels], refs[n_panels], refs[n_panels + 1 : -4]
    ham_buf, panel_buf, acc, sems = refs[-4:]

    def issue(entry, carry):
        chunk, i = lax.shift_right_logical(entry, 2), entry & 3
        source = ham.at[table[HAM_AT + entry]]
        pltpu.make_async_copy(source, ham_buf.at[chunk, i], sems.at[0, chunk]).start()
        place = table[PLACE_AT + entry]

        def copy(ref, index):
            pltpu.make_async_copy(ref.at[index], panel_buf.at[chunk, i], sems.at[1, chunk]).start()

        if n_panels == 1:
            copy(panels[0], place)
        else:
            for k, ref in enumerate(panels):
                pl.when(lax.shift_right_logical(place, 3) == k)(functools.partial(copy, ref, place & 7))
        return carry

    lax.fori_loop(0, table[COUNT_AT], issue, 0)
    acc[...] = jnp.zeros_like(acc)
    zero = jnp.zeros((128, 128), jnp.bfloat16)

    def work(chunk, carry):
        pltpu.make_async_copy(ham_buf.at[chunk], ham_buf.at[chunk], sems.at[0, chunk]).wait()
        pltpu.make_async_copy(panel_buf.at[chunk], panel_buf.at[chunk], sems.at[1, chunk]).wait()
        sums = []
        for i in range(4):
            x, t = panel_buf[chunk, i, 0], panel_buf[chunk, i, 1]
            left = jnp.concatenate([ham_buf[chunk, i, 0], ham_buf[chunk, i, 1]], axis=1)
            top = jnp.concatenate([x, t], axis=1)
            right = jnp.concatenate([top, jnp.concatenate([zero, x], axis=1)], axis=0)
            sums.append(jnp.dot(left, right, preferred_element_type=jnp.float32))
        for i in range(4):
            acc[table[OUT_AT + chunk * 4 + i]] += sums[i]
        return carry

    lax.fori_loop(0, lax.shift_right_logical(table[COUNT_AT], 2), work, 0)

    for out in range(8):
        scale = table[KEEP_AT + out].astype(jnp.float32)
        for kind in range(2):
            total = acc[out, :, 128 * kind : 128 * (kind + 1)]
            value = scale * (2.0 * total - old[out, kind].astype(jnp.float32))
            if apart:
                new[kind][out] = value.astype(jnp.bfloat16)
            else:
                new[0][out, kind] = value.astype(jnp.bfloat16)


def combine(table, ham, panels, old, apart):
    one = jax.ShapeDtypeStruct((8, 128, 128), jnp.bfloat16)
    both = jax.ShapeDtypeStruct(old.shape, jnp.bfloat16)
    return pl.pallas_call(
        functools.partial(combine_kernel, len(panels), apart),
        out_shape=(one, one) if apart else both,
        in_specs=[SMEM, HBM] + [HBM] * len(panels) + [VMEM],
        out_specs=(VMEM, VMEM) if apart else VMEM,
        scratch_shapes=[
            pltpu.VMEM((16, 4, 2, 128, 128), jnp.bfloat16),
            pltpu.VMEM((16, 4, 2, 128, 128), jnp.bfloat16),
            pltpu.VMEM((9, 128, 256), jnp.float32),
            pltpu.SemaphoreType.DMA((2, 16)),
        ],
        compiler_params=pltpu.CompilerParams(vmem_limit_bytes=VMEM_BYTES),
        cost_estimate=pl.CostEstimate(flops=1 << 30, bytes_accessed=1 << 23, transcendentals=0),
    )(table, ham, *panels, old)


def pack_kernel(table, *refs):
    panels, packed, sem = refs[:SIDE], refs[SIDE : SIDE + 3], refs[SIDE + 3]

    def copy(ref, index, out, i, slot):
        return pltpu.make_async_copy(ref.at[index], out.at[i], sem.at[slot])

    for wait in (False, True):
        for b, out in enumerate(packed):

            def step(i, carry, b=b, out=out, wait=wait):
                slot = b * CAP + i
                place = table[slot]
                if wait:
                    copy(panels[0], 0, out, i, slot).wait()
                else:
                    for a, ref in enumerate(panels):

                        @pl.when(lax.shift_right_logical(place, 3) == a)
                        def _(ref=ref):
                            copy(ref, place & 7, out, i, slot).start()

                return carry

            lax.fori_loop(0, table[3 * CAP + b], step, 0)


def pack(table, panels):
    shape = jax.ShapeDtypeStruct((CAP, 2, 128, 128), jnp.bfloat16)
    return pl.pallas_call(
        pack_kernel,
        out_shape=(shape,) * 3,
        in_specs=[SMEM] + [ANY] * SIDE,
        out_specs=(VMEM,) * 3,
        scratch_shapes=[pltpu.SemaphoreType.DMA((3 * CAP,))],
        compiler_params=pltpu.CompilerParams(vmem_limit_bytes=VMEM_BYTES),
        cost_estimate=pl.CostEstimate(flops=0, bytes_accessed=1 << 22, transcendentals=0),
    )(table, *panels)


def position():
    layer, row_group, col = (lax.axis_index(name) for name in ("depth", "row", "col"))
    at_y, at_x = lax.shift_right_logical(row_group, 2), row_group & 3
    return layer, row_group, col, jnp.where(layer == 0, at_x, at_y), jnp.where(layer == 0, at_y, at_x)


def slots_of_rows(rows, layer, slot_of):
    def fill(slot, carry):
        for column in range(2):
            slot_of[column * 512 + rows[2 * layer + column, slot]] = slot
        return carry

    lax.fori_loop(0, 64, fill, 0)


def split(i):
    return lax.shift_right_logical(i, 5), lax.shift_right_logical(i, 3) & 3, i & 7


def coordinates(slot, layer):
    y, x = lax.shift_right_logical(slot, 4), lax.shift_right_logical(slot, 2) & 3
    return jnp.where(layer == 0, x, y), jnp.where(layer == 0, y, x)


def needs_kernel(rows, cols, other_cols, keep, *refs):
    tables, flag, slot_of, counts = refs[:3], refs[3], refs[4], refs[5]
    layer, row_group, col, first, second = position()
    slots_of_rows(rows, layer, slot_of)
    for i in range(5):
        counts[i] = 0

    def put(at, ham, out, places):
        for table, place in zip(tables, places, strict=True):
            table[HAM_AT + at] = ham
            table[OUT_AT + at] = out
            table[PLACE_AT + at] = place

    def look(i, carry):
        column, t, q = split(i)
        group = lax.shift_right_logical(t, 1)
        row = rows[2 * layer + column, 4 * row_group + t] - 32 * row_group - 16 * group
        wanted = jnp.where(group == layer, cols[row, q], other_cols[row, q])
        slot = slot_of[column * 512 + wanted] & 63

        @pl.when((rows[2 * layer + column, slot] == wanted) & (keep[2 * layer + column, t] != 0))
        def _():
            at_first, at_second = coordinates(slot, layer)
            sender = (second - at_second) & 3
            rank = counts[sender]
            counts[sender] = rank + 1
            index = column * 4 + (slot & 3)
            near = ((at_first - first) & 3) * 8 + index
            n = counts[4]
            counts[4] = n + 1
            sparse = jnp.where(sender == 0, near, (sender + 3) * 8 + rank)
            places = (((4 - sender) & 3) * 32 + near, sparse, lax.shift_right_logical(slot, 2) * 8 + index)
            put(n, (q * 2 + group) * 16 + row, lax.shift_right_logical(i, 3), places)

        return carry

    lax.fori_loop(0, 64, look, 0)
    flag[0] = jnp.where((counts[1] > CAP) | (counts[2] > CAP) | (counts[3] > CAP), 1, 0)
    n = counts[4]
    padded = (n + 3) & ~3

    def pad(i, carry):
        put(i, 0, 8, (0, 0, 0))
        return carry

    lax.fori_loop(n, padded, pad, 0)
    for table in tables:
        table[COUNT_AT] = padded
        for out in range(8):
            table[KEEP_AT + out] = keep[2 * layer + out // 4, out % 4]


def needs(cheb_rows, ham_cols, other_cols, keep_mask):
    table = jax.ShapeDtypeStruct((208,), jnp.int32)
    return pl.pallas_call(
        needs_kernel,
        out_shape=(table,) * 3 + (jax.ShapeDtypeStruct((1,), jnp.int32),),
        in_specs=[SMEM] * 4,
        out_specs=(SMEM,) * 4,
        scratch_shapes=[pltpu.SMEM((size,), jnp.int32) for size in (1024, 8)],
    )(cheb_rows, ham_cols, other_cols, keep_mask)


def sends_kernel(rows, *refs):
    known, (table, slot_of, count) = refs[:3], refs[3:]
    layer, row_group, col, first, second = position()
    slots_of_rows(rows, layer, slot_of)
    for b, theirs in enumerate(known):
        to_second = (second + 1 + b) & 3
        to_row = jnp.where(layer == 0, to_second * SIDE + first, first * SIDE + to_second)
        count[0] = 0

        def look(i, carry, b=b, theirs=theirs, to_row=to_row):
            column, t, q = split(i)
            group = lax.shift_right_logical(t, 1)
            row = rows[2 * layer + column, 4 * to_row + t] - 32 * to_row - 16 * group
            wanted = theirs[jnp.where(group == layer, 0, 16) + row, q]
            slot = slot_of[column * 512 + wanted] & 63
            at = (2 * layer + column) * 4 + t
            kept = theirs[32 + lax.shift_right_logical(at, 3), at & 7] != 0
            at_first, at_second = coordinates(slot, layer)

            @pl.when((rows[2 * layer + column, slot] == wanted) & kept & (at_second == second))
            def _():
                rank = count[0]
                count[0] = rank + 1

                @pl.when(rank < CAP)
                def _():
                    table[b * CAP + rank] = ((at_first - first) & 3) * 8 + column * 4 + (slot & 3)

            return carry

        lax.fori_loop(0, 64, look, 0)
        table[3 * CAP + b] = jnp.minimum(count[0], CAP)


def sends(cheb_rows, known):
    return pl.pallas_call(
        sends_kernel,
        out_shape=jax.ShapeDtypeStruct((32,), jnp.int32),
        in_specs=[SMEM] * 4,
        out_specs=SMEM,
        scratch_shapes=[pltpu.SMEM((1024,), jnp.int32), pltpu.SMEM((1,), jnp.int32)],
    )(cheb_rows, *known)


def on_device(
    ham_blocks,
    deriv_blocks,
    ham_cols,
    cheb_prev,
    cheb_cur,
    tang_prev,
    tang_cur,
    cheb_rows,
    keep_mask,
):
    layer = lax.axis_index("depth")

    def mine(array):
        return lax.dynamic_slice_in_dim(array, 2 * layer, 2, 0)

    def paired(cheb, tang):
        return jnp.stack([mine(cheb).reshape(8, 128, 128), mine(tang).reshape(8, 128, 128)], axis=1)

    ham_pair = jnp.stack([ham_blocks[:, 0], deriv_blocks[:, 0]], axis=1)
    ham = lax.all_gather(ham_pair, ("col", "depth"), axis=0, tiled=True)

    other_cols = swap(ham_cols)
    ring_table, sparse_table, dense_table, overflow = needs(cheb_rows, ham_cols, other_cols, keep_mask)
    flags = lax.all_to_all(jnp.broadcast_to(overflow, (256, 1, 128)), AXES, 0, 0, tiled=True)
    known = jnp.concatenate([ham_cols, other_cols, keep_mask.reshape(2, 8)])
    pack_table = sends(cheb_rows, [shift_side(known, SIDE - b, True) for b in (1, 2, 3)])

    def nearby(piece):
        return [piece] + [shift_side(piece, SIDE - a, False) for a in (1, 2, 3)]

    def ring_panel(piece, ready):
        here = nearby(piece)
        after = [shift_side(piece, SIDE - 1, True) for piece in here]
        before = [shift_side(piece, 1, True) for piece in here]
        last, ready = lax.optimization_barrier((after[0], ready))
        across = [shift_side(piece, SIDE - 1, True) for piece in (last, after[1])]
        across += [shift_side(piece, 1, True) for piece in before[2:]]
        return here + after + across + before, ready

    def sparse_step(ham, now, old):
        near_pieces = nearby(now)
        packed = pack(pack_table, near_pieces)
        arrived = [shift_side(packed[b - 1], b, True) for b in (1, 2, 3)]
        return combine(sparse_table, ham, near_pieces + arrived, old, True)

    def dense_step(ham, now, old):
        panel = lax.all_gather(now, "row", axis=0, tiled=True)
        return combine(dense_table, ham, [panel], old, True)

    now = paired(cheb_cur, tang_cur)
    panel, (flags, pack_table) = ring_panel(now, (flags, pack_table))
    crowded = jnp.max(flags) > 0
    middle = combine(ring_table, ham, panel, paired(cheb_prev, tang_prev), False)
    last = lax.cond(crowded, dense_step, sparse_step, ham, middle, now)

    def whole(mine):
        theirs = swap(mine)
        both = jnp.stack([jnp.where(layer == 0, mine, theirs), jnp.where(layer == 0, theirs, mine)])
        return both.reshape(4, 4, 128, 128)

    return whole(last[0]), whole(last[1])


def solution(mesh):
    placed = (
        P(("row", "depth"), "col", None, None),
        P(("row", "depth"), "col", None, None),
        P(("row", "depth"), None),
        P("col", "row", None, None),
        P("col", "row", None, None),
        P("col", "row", None, None),
        P("col", "row", None, None),
        P("col", None),
        P("col", "row"),
    )
    return jax.shard_map(
        on_device,
        mesh=mesh,
        in_specs=placed,
        out_specs=(P("col", "row", None, None), P("col", "row", None, None)),
        check_vma=False,
    )
```

```python
import functools

import jax
import jax.numpy as jnp
from jax import lax
from jax.experimental import pallas as pl
from jax.experimental.pallas import tpu as pltpu
from jax.sharding import PartitionSpec as P

ROWS, COLS, CORES = 16, 8, 2
SIDE = 4
CAP = 8
VMEM_BYTES = 56 * 1024 * 1024
AXES = ("row", "col", "depth")
HBM = pl.BlockSpec(memory_space=pltpu.HBM)
VMEM = pl.BlockSpec(memory_space=pltpu.VMEM)
SMEM = pl.BlockSpec(memory_space=pltpu.SMEM)
ANY = pl.BlockSpec(memory_space=pl.ANY)
HAM_AT, PLACE_AT, OUT_AT, KEEP_AT, COUNT_AT = 0, 64, 128, 192, 200


def side_ring(shift, second):
    pairs = []
    for y in range(SIDE):
        for x in range(SIDE):
            for core in range(CORES):
                along_x = (core == 0) != second
                to_y = y if along_x else (y + shift) % SIDE
                to_x = (x + shift) % SIDE if along_x else x
                pairs.append(((y * SIDE + x) * CORES + core, (to_y * SIDE + to_x) * CORES + core))
    return pairs


def shift_side(array, shift, second):
    return lax.ppermute(array, ("row", "depth"), side_ring(shift, second))


def swap(array):
    return lax.ppermute(array, "depth", [(0, 1), (1, 0)])


def combine_kernel(n_panels, apart, table, ham, *refs):
    panels, old, new = refs[:n_panels], refs[n_panels], refs[n_panels + 1 : -4]
    ham_buf, panel_buf, acc, sems = refs[-4:]

    def issue(entry, carry):
        chunk, i = lax.shift_right_logical(entry, 2), entry & 3
        for kind in range(2):
            source = ham.at[table[HAM_AT + entry] + 16 * kind]
            pltpu.make_async_copy(source, ham_buf.at[chunk, i, kind], sems.at[0, chunk]).start()
        place = table[PLACE_AT + entry]

        def copy(ref, index):
            pltpu.make_async_copy(ref.at[index], panel_buf.at[chunk, i], sems.at[1, chunk]).start()

        if n_panels == 1:
            copy(panels[0], place)
        else:
            for k, ref in enumerate(panels):
                pl.when(lax.shift_right_logical(place, 3) == k)(functools.partial(copy, ref, place & 7))
        return carry

    lax.fori_loop(0, table[COUNT_AT], issue, 0)
    acc[...] = jnp.zeros_like(acc)
    zero = jnp.zeros((128, 128), jnp.bfloat16)

    def work(chunk, carry):
        pltpu.make_async_copy(ham_buf.at[chunk], ham_buf.at[chunk], sems.at[0, chunk]).wait()
        pltpu.make_async_copy(panel_buf.at[chunk], panel_buf.at[chunk], sems.at[1, chunk]).wait()
        sums = []
        for i in range(4):
            x, t = panel_buf[chunk, i, 0], panel_buf[chunk, i, 1]
            left = jnp.concatenate([ham_buf[chunk, i, 0], ham_buf[chunk, i, 1]], axis=1)
            top = jnp.concatenate([x, t], axis=1)
            right = jnp.concatenate([top, jnp.concatenate([zero, x], axis=1)], axis=0)
            sums.append(jnp.dot(left, right, preferred_element_type=jnp.float32))
        for i in range(4):
            acc[table[OUT_AT + chunk * 4 + i]] += sums[i]
        return carry

    lax.fori_loop(0, lax.shift_right_logical(table[COUNT_AT], 2), work, 0)

    for out in range(8):
        scale = table[KEEP_AT + out].astype(jnp.float32)
        for kind in range(2):
            total = acc[out, :, 128 * kind : 128 * (kind + 1)]
            value = scale * (2.0 * total - old[out, kind].astype(jnp.float32))
            if apart:
                new[kind][out] = value.astype(jnp.bfloat16)
            else:
                new[0][out, kind] = value.astype(jnp.bfloat16)


def combine(table, ham, panels, old, apart):
    one = jax.ShapeDtypeStruct((8, 128, 128), jnp.bfloat16)
    both = jax.ShapeDtypeStruct(old.shape, jnp.bfloat16)
    return pl.pallas_call(
        functools.partial(combine_kernel, len(panels), apart),
        out_shape=(one, one) if apart else both,
        in_specs=[SMEM, HBM] + [HBM] * len(panels) + [VMEM],
        out_specs=(VMEM, VMEM) if apart else VMEM,
        scratch_shapes=[
            pltpu.VMEM((16, 4, 2, 128, 128), jnp.bfloat16),
            pltpu.VMEM((16, 4, 2, 128, 128), jnp.bfloat16),
            pltpu.VMEM((9, 128, 256), jnp.float32),
            pltpu.SemaphoreType.DMA((2, 16)),
        ],
        compiler_params=pltpu.CompilerParams(vmem_limit_bytes=VMEM_BYTES),
        cost_estimate=pl.CostEstimate(flops=1 << 30, bytes_accessed=1 << 23, transcendentals=0),
    )(table, ham, *panels, old)


def pack_kernel(table, *refs):
    panels, packed, sem = refs[:SIDE], refs[SIDE : SIDE + 3], refs[SIDE + 3]

    def copy(ref, index, out, i, slot):
        return pltpu.make_async_copy(ref.at[index], out.at[i], sem.at[slot])

    for wait in (False, True):
        for b, out in enumerate(packed):

            def step(i, carry, b=b, out=out, wait=wait):
                slot = b * CAP + i
                place = table[slot]
                if wait:
                    copy(panels[0], 0, out, i, slot).wait()
                else:
                    for a, ref in enumerate(panels):

                        @pl.when(lax.shift_right_logical(place, 3) == a)
                        def _(ref=ref):
                            copy(ref, place & 7, out, i, slot).start()

                return carry

            lax.fori_loop(0, table[3 * CAP + b], step, 0)


def pack(table, panels):
    shape = jax.ShapeDtypeStruct((CAP, 2, 128, 128), jnp.bfloat16)
    return pl.pallas_call(
        pack_kernel,
        out_shape=(shape,) * 3,
        in_specs=[SMEM] + [ANY] * SIDE,
        out_specs=(VMEM,) * 3,
        scratch_shapes=[pltpu.SemaphoreType.DMA((3 * CAP,))],
        compiler_params=pltpu.CompilerParams(vmem_limit_bytes=VMEM_BYTES),
        cost_estimate=pl.CostEstimate(flops=0, bytes_accessed=1 << 22, transcendentals=0),
    )(table, *panels)


def position():
    layer, row_group, col = (lax.axis_index(name) for name in ("depth", "row", "col"))
    at_y, at_x = lax.shift_right_logical(row_group, 2), row_group & 3
    return layer, row_group, col, jnp.where(layer == 0, at_x, at_y), jnp.where(layer == 0, at_y, at_x)


def slots_of_rows(rows, layer, slot_of):
    def fill(slot, carry):
        for column in range(2):
            slot_of[column * 512 + rows[2 * layer + column, slot]] = slot
        return carry

    lax.fori_loop(0, 64, fill, 0)


def split(i):
    return lax.shift_right_logical(i, 5), lax.shift_right_logical(i, 3) & 3, i & 7


def coordinates(slot, layer):
    y, x = lax.shift_right_logical(slot, 4), lax.shift_right_logical(slot, 2) & 3
    return jnp.where(layer == 0, x, y), jnp.where(layer == 0, y, x)


def needs_kernel(rows, cols, other_cols, keep, *refs):
    tables, flag, slot_of, counts = refs[:3], refs[3], refs[4], refs[5]
    layer, row_group, col, first, second = position()
    slots_of_rows(rows, layer, slot_of)
    for i in range(5):
        counts[i] = 0

    def put(at, ham, out, places):
        for table, place in zip(tables, places, strict=True):
            table[HAM_AT + at] = ham
            table[OUT_AT + at] = out
            table[PLACE_AT + at] = place

    def look(i, carry):
        column, t, q = split(i)
        group = lax.shift_right_logical(t, 1)
        row = rows[2 * layer + column, 4 * row_group + t] - 32 * row_group - 16 * group
        wanted = jnp.where(group == layer, cols[row, q], other_cols[row, q])
        slot = slot_of[column * 512 + wanted] & 63

        @pl.when((rows[2 * layer + column, slot] == wanted) & (keep[2 * layer + column, t] != 0))
        def _():
            at_first, at_second = coordinates(slot, layer)
            sender = (second - at_second) & 3
            rank = counts[sender]
            counts[sender] = rank + 1
            index = column * 4 + (slot & 3)
            near = ((at_first - first) & 3) * 8 + index
            n = counts[4]
            counts[4] = n + 1
            sparse = jnp.where(sender == 0, near, (sender + 3) * 8 + rank)
            places = (((4 - sender) & 3) * 32 + near, sparse, lax.shift_right_logical(slot, 2) * 8 + index)
            put(n, (q * 2 + group) * 32 + row, lax.shift_right_logical(i, 3), places)

        return carry

    lax.fori_loop(0, 64, look, 0)
    flag[0] = jnp.where((counts[1] > CAP) | (counts[2] > CAP) | (counts[3] > CAP), 1, 0)
    n = counts[4]
    padded = (n + 3) & ~3

    def pad(i, carry):
        put(i, 0, 8, (0, 0, 0))
        return carry

    lax.fori_loop(n, padded, pad, 0)
    for table in tables:
        table[COUNT_AT] = padded
        for out in range(8):
            table[KEEP_AT + out] = keep[2 * layer + out // 4, out % 4]


def needs(cheb_rows, ham_cols, other_cols, keep_mask):
    table = jax.ShapeDtypeStruct((208,), jnp.int32)
    return pl.pallas_call(
        needs_kernel,
        out_shape=(table,) * 3 + (jax.ShapeDtypeStruct((1,), jnp.int32),),
        in_specs=[SMEM] * 4,
        out_specs=(SMEM,) * 4,
        scratch_shapes=[pltpu.SMEM((size,), jnp.int32) for size in (1024, 8)],
    )(cheb_rows, ham_cols, other_cols, keep_mask)


def sends_kernel(rows, *refs):
    known, (table, slot_of, count) = refs[:3], refs[3:]
    layer, row_group, col, first, second = position()
    slots_of_rows(rows, layer, slot_of)
    for b, theirs in enumerate(known):
        to_second = (second + 1 + b) & 3
        to_row = jnp.where(layer == 0, to_second * SIDE + first, first * SIDE + to_second)
        count[0] = 0

        def look(i, carry, b=b, theirs=theirs, to_row=to_row):
            column, t, q = split(i)
            group = lax.shift_right_logical(t, 1)
            row = rows[2 * layer + column, 4 * to_row + t] - 32 * to_row - 16 * group
            wanted = theirs[jnp.where(group == layer, 0, 16) + row, q]
            slot = slot_of[column * 512 + wanted] & 63
            at = (2 * layer + column) * 4 + t
            kept = theirs[32 + lax.shift_right_logical(at, 3), at & 7] != 0
            at_first, at_second = coordinates(slot, layer)

            @pl.when((rows[2 * layer + column, slot] == wanted) & kept & (at_second == second))
            def _():
                rank = count[0]
                count[0] = rank + 1

                @pl.when(rank < CAP)
                def _():
                    table[b * CAP + rank] = ((at_first - first) & 3) * 8 + column * 4 + (slot & 3)

            return carry

        lax.fori_loop(0, 64, look, 0)
        table[3 * CAP + b] = jnp.minimum(count[0], CAP)


def sends(cheb_rows, known):
    return pl.pallas_call(
        sends_kernel,
        out_shape=jax.ShapeDtypeStruct((32,), jnp.int32),
        in_specs=[SMEM] * 4,
        out_specs=SMEM,
        scratch_shapes=[pltpu.SMEM((1024,), jnp.int32), pltpu.SMEM((1,), jnp.int32)],
    )(cheb_rows, *known)


def on_device(
    ham_blocks,
    deriv_blocks,
    ham_cols,
    cheb_prev,
    cheb_cur,
    tang_prev,
    tang_cur,
    cheb_rows,
    keep_mask,
):
    layer = lax.axis_index("depth")

    def mine(array):
        return lax.dynamic_slice_in_dim(array, 2 * layer, 2, 0)

    def paired(cheb, tang):
        return jnp.stack([mine(cheb).reshape(8, 128, 128), mine(tang).reshape(8, 128, 128)], axis=1)

    ham_pair = jnp.concatenate([ham_blocks[:, 0], deriv_blocks[:, 0]])
    ham = lax.all_gather(ham_pair, ("col", "depth"), axis=0, tiled=True)

    other_cols = swap(ham_cols)
    ring_table, sparse_table, dense_table, overflow = needs(cheb_rows, ham_cols, other_cols, keep_mask)
    flags = lax.all_to_all(jnp.broadcast_to(overflow, (256, 1, 128)), AXES, 0, 0, tiled=True)
    known = jnp.concatenate([ham_cols, other_cols, keep_mask.reshape(2, 8)])
    pack_table = sends(cheb_rows, [shift_side(known, SIDE - b, True) for b in (1, 2, 3)])

    def nearby(piece):
        return [piece] + [shift_side(piece, SIDE - a, False) for a in (1, 2, 3)]

    def ring_panel(piece, ready):
        here = nearby(piece)
        after = [shift_side(piece, SIDE - 1, True) for piece in here]
        before = [shift_side(piece, 1, True) for piece in here]
        last, ready = lax.optimization_barrier((after[0], ready))
        across = [shift_side(piece, SIDE - 1, True) for piece in (last, after[1])]
        across += [shift_side(piece, 1, True) for piece in before[2:]]
        return here + after + across + before, ready

    def sparse_step(ham, now, old):
        near_pieces = nearby(now)
        packed = pack(pack_table, near_pieces)
        arrived = [shift_side(packed[b - 1], b, True) for b in (1, 2, 3)]
        return combine(sparse_table, ham, near_pieces + arrived, old, True)

    def dense_step(ham, now, old):
        panel = lax.all_gather(now, "row", axis=0, tiled=True)
        return combine(dense_table, ham, [panel], old, True)

    now = paired(cheb_cur, tang_cur)
    panel, (flags, pack_table) = ring_panel(now, (flags, pack_table))
    crowded = jnp.max(flags) > 0
    middle = combine(ring_table, ham, panel, paired(cheb_prev, tang_prev), False)
    last = lax.cond(crowded, dense_step, sparse_step, ham, middle, now)

    def whole(mine):
        theirs = swap(mine)
        both = jnp.stack([jnp.where(layer == 0, mine, theirs), jnp.where(layer == 0, theirs, mine)])
        return both.reshape(4, 4, 128, 128)

    return whole(last[0]), whole(last[1])


def solution(mesh):
    placed = (
        P(("row", "depth"), "col", None, None),
        P(("row", "depth"), "col", None, None),
        P(("row", "depth"), None),
        P("col", "row", None, None),
        P("col", "row", None, None),
        P("col", "row", None, None),
        P("col", "row", None, None),
        P("col", None),
        P("col", "row"),
    )
    return jax.shard_map(
        on_device,
        mesh=mesh,
        in_specs=placed,
        out_specs=(P("col", "row", None, None), P("col", "row", None, None)),
        check_vma=False,
    )
```
